256 devices in a mesh: win: 32 (over y, z), pos: 8 (over x, core).
Axes of the slice: x: 4, y: 4, z: 8, core: 2. Of those that a mesh axis runs over, the one named last changes fastest.
Arguments:
- tokens: bfloat16 [256, 128, 2560], P('win'), may hold values from -6 to 6
- keep_index: int32 [256, 128], P('win'), may hold values from 0 to 255, as said below
- norm_gain: float32 [2560], replicated, may hold values from 0.5 to 1.5
- w_qkv: bfloat16 [3, 2560, 2560], P(None, 'pos'), may hold values from -0.125 to 0.125
- w_out: bfloat16 [2560, 2560], P('pos'), may hold values from -1 to 1
Outputs:
- mixed: bfloat16 [256, 128, 2560], P('win', 'pos')
The draws below stay inside these ranges and needn't reach their ends.
Inputs may be any that keep to these rules, and one draw needn't show every extreme that they name: keep_index[w, j] is 2 j or 2 j + 1: each window keeps exactly one position of every aligned pair of positions.
All inputs are finite; a program needn't handle non-finite values.
Results may differ from the reference program's by a relative error of at most 0.019.
Values may be sent and summed in bfloat16 or wider, within the bound.
No kernel may reach another device: no remote copies, remote signals or barrier semaphores. Data moves between devices by JAX's collectives and lax.ppermute only.
A program may use at most 128 MiB of HBM per device.

```python
import math
import jax
import jax.numpy as jnp
from jax import lax

D = 2560
HEADS = 16
POSITIONS = 256
KEEP = 128
WINDOWS = 256
N_POS = 8


def draw_keep_index(key, part):
    key = jax.random.fold_in(key, 7)
    choose_bits = jax.random.randint(key, (WINDOWS, KEEP), 0, 2, dtype=jnp.int32)
    pair_starts = 2 * jnp.arange(KEEP, dtype=jnp.int32)[None, :]
    return (pair_starts + choose_bits).astype(jnp.int32)


def block_scale(rng, shape, pieces, least, top_value):
    gain, own = 1.0, jax.random.fold_in(rng, 6)
    for position, shards_of in pieces:
        draws = jnp.exp(jax.random.uniform(jax.random.fold_in(own, position), (shards_of,), jnp.float32, least / len(pieces), top_value / len(pieces)))
        gain = gain * jnp.repeat(draws, shape[position] // shards_of).reshape([-1 if axis == position else 1 for axis in range(len(shape))])
    return gain


def gaussian(key, shape, width, limit, pieces=(), kind=jnp.bfloat16):
    level = block_scale(key, shape, pieces, -0.22, 0.18) if pieces else 1.0
    drawn = jax.random.normal(key, shape, jnp.float32) * width * level
    return jnp.minimum(jnp.maximum(drawn, -limit), limit).astype(kind)


def setup_inputs(seed: int = 0) -> dict:
    splits = jax.random.split(jax.random.key(seed), 6)
    tokens = gaussian(splits[0], (WINDOWS, KEEP, D), 1.0, 6.0, ((0, 32),))
    keep_index = draw_keep_index(jax.random.fold_in(splits[5], 71), 0)
    norm_gain = jnp.clip(1.0 + 0.1 * jax.random.normal(splits[2], (D,), jnp.float32), 0.5, 1.5)
    w_qkv = gaussian(splits[3], (3, D, D), D ** -0.5, 0.125, ((1, 8),))
    w_out = gaussian(splits[4], (D, D), (D // 64) ** -0.5, 1.0, ((0, 8),))
    return {"tokens": tokens, "keep_index": keep_index, "norm_gain": norm_gain, "w_qkv": w_qkv, "w_out": w_out}


NORM_EPSILON = 1e-05

def reference(tokens, keep_index, norm_gain, w_qkv, w_out):
    activations = tokens.astype(jnp.float32)
    average = lax.optimization_barrier(jnp.mean(activations, axis=-1, keepdims=True))
    centered = activations - average
    variance = lax.optimization_barrier(jnp.mean(centered * centered, axis=-1, keepdims=True))
    normed = (centered * lax.rsqrt(variance + NORM_EPSILON) * norm_gain.astype(jnp.float32)).astype(jnp.bfloat16)
    flat_normed = normed.reshape(WINDOWS * KEEP, D)
    group_width = D // N_POS
    head_dim = D // HEADS
    head_local = HEADS // N_POS
    score_scale = 1.0 / math.sqrt(head_dim)
    window_rows = jnp.arange(WINDOWS, dtype=jnp.int32)[:, None]
    kept = jnp.zeros((WINDOWS, POSITIONS), jnp.float32).at[window_rows, keep_index].set(1.0)
    key_mask = kept.T[:, None, None, :]
    query_kept = kept.T[:, None, :]

    def one_group(group_index, running):
        first = (group_index * group_width).astype(jnp.int32)
        weights = lax.dynamic_slice_in_dim(w_qkv, first, group_width, 1).reshape(3 * group_width, D)
        projected = jnp.dot(flat_normed, weights.T, preferred_element_type=jnp.float32).astype(jnp.bfloat16)
        projected = projected.reshape(WINDOWS, KEEP, 3 * group_width)
        spread_qkv = jnp.zeros((WINDOWS, POSITIONS, 3 * group_width), jnp.bfloat16).at[window_rows, keep_index].set(projected)
        spread_qkv = spread_qkv.reshape(WINDOWS, POSITIONS, 3, head_local, head_dim).astype(jnp.float32)
        scores = jnp.einsum('wphd,uphd->phwu', spread_qkv[:, :, 0], spread_qkv[:, :, 1]) * score_scale
        exponent = jnp.exp(scores) * key_mask
        denominator = lax.optimization_barrier(jnp.sum(exponent, axis=-1)) + 1.0 - query_kept
        attn_weights = (exponent / denominator[..., None]).astype(jnp.bfloat16)
        attended = jnp.einsum('phwu,uphd->wphd', attn_weights.astype(jnp.float32), spread_qkv[:, :, 2]).astype(jnp.bfloat16)
        kept_attended = attended[window_rows, keep_index].reshape(WINDOWS * KEEP, group_width)
        out_rows = lax.dynamic_slice_in_dim(w_out, first, group_width, 0)
        group_term = jnp.dot(kept_attended, out_rows, preferred_element_type=jnp.float32).astype(jnp.bfloat16)
        group_term = lax.optimization_barrier(group_term).astype(jnp.float32)
        return running + group_term.reshape(WINDOWS, KEEP, D)
    summed = lax.fori_loop(0, N_POS, one_group, jnp.zeros((WINDOWS, KEEP, D), jnp.float32))
    return (activations + summed).astype(jnp.bfloat16)
```

```python
import math

import jax
import jax.numpy as jnp
from jax import lax
from jax.experimental import pallas as pl
from jax.experimental.pallas import tpu as pltpu
from jax.sharding import PartitionSpec as P

D = 2560
HEADS = 16
HEAD_DIM = D // HEADS
POSITIONS = 256
PAIRS = POSITIONS // 2
NORM_EPSILON = 1e-05
SLOT = 512
FLAG = 3 * HEAD_DIM

F32 = jnp.float32
BF16 = jnp.bfloat16


def project_kernel(tokens_ref, keep_ref, gain_ref, w_hbm, out_ref, w_ref, rows_ref, sems):
    step = pl.program_id(0)
    windows, pairs, _ = tokens_ref.shape
    rows = windows * pairs

    def copies():
        made = []
        for head in range(2):
            for c in range(3):
                made.append(pltpu.make_async_copy(
                    w_hbm.at[c, pl.ds(head * HEAD_DIM, HEAD_DIM)],
                    w_ref.at[pl.ds(head * SLOT + c * HEAD_DIM, HEAD_DIM)],
                    sems.at[head * 3 + c],
                ))
        return made

    @pl.when(step == 0)
    def _():
        for copy in copies():
            copy.start()
        for head in range(2):
            w_ref[head * SLOT + FLAG:(head + 1) * SLOT, :] = jnp.zeros((SLOT - FLAG, D), BF16)

    for w in range(windows):
        x = tokens_ref[w].astype(F32)
        mean = jnp.sum(x, axis=-1, keepdims=True) * (1.0 / D)
        centered = x - mean
        variance = jnp.sum(centered * centered, axis=-1, keepdims=True) * (1.0 / D)
        normed = centered * lax.rsqrt(variance + NORM_EPSILON) * gain_ref[...]
        for c in range(D // 128):
            rows_ref[c, pl.ds(w, pairs, stride=windows), :] = normed[:, c * 128:(c + 1) * 128]

    @pl.when(step == 0)
    def _():
        for copy in copies():
            copy.wait()

    projected = lax.dot_general(
        jnp.concatenate([rows_ref[c].astype(BF16) for c in range(D // 128)], axis=-1),
        w_ref[...],
        (((1,), (1,)), ((), ())),
        preferred_element_type=F32,
    )
    parity = (keep_ref[...] & 1).astype(F32)
    row = lax.broadcasted_iota(jnp.int32, (rows, windows), 0)
    pick_window = (row % windows == lax.broadcasted_iota(jnp.int32, (rows, windows), 1)).astype(F32)
    spread = jnp.dot(pick_window, parity, preferred_element_type=F32)
    row_pair = lax.broadcasted_iota(jnp.int32, spread.shape, 0) // windows + step * pairs
    mine = row_pair == lax.broadcasted_iota(jnp.int32, spread.shape, 1)
    odd = jnp.sum(jnp.where(mine, spread, 0.0), axis=-1, keepdims=True)
    tail_lane = lax.broadcasted_iota(jnp.int32, (rows, 128), 1)
    first_flag = FLAG - (SLOT - 128)
    for head in range(2):
        part = projected[:, head * SLOT:(head + 1) * SLOT]
        tail = part[:, SLOT - 128:]
        tail = jnp.where(tail_lane == first_flag, odd, jnp.where(tail_lane == first_flag + 1, 1.0 - odd, tail))
        blocks = pairs // 16
        for b in range(blocks):
            lo, hi = b * 16 * windows, (b + 1) * 16 * windows
            out_ref[head, :, b, :, :SLOT - 128] = (
                part[lo:hi, :SLOT - 128].reshape(16, windows, SLOT - 128).astype(BF16)
            )
            out_ref[head, :, b, :, SLOT - 128:] = tail[lo:hi].reshape(16, windows, 128).astype(BF16)


def project(tokens, keep_index, norm_gain, w_qkv):
    windows, keep, _ = tokens.shape
    pos_count = 8
    blocks_per_step = 2
    pairs = 16 * blocks_per_step
    return pl.pallas_call(
        project_kernel,
        grid=(keep // pairs,),
        in_specs=[
            pl.BlockSpec((windows, pairs, D), lambda s: (0, s, 0)),
            pl.BlockSpec((windows, keep), lambda s: (0, 0)),
            pl.BlockSpec((1, D), lambda s: (0, 0)),
            pl.BlockSpec(memory_space=pl.ANY),
        ],
        out_specs=pl.BlockSpec((2, 16, blocks_per_step, windows, SLOT), lambda s: (0, 0, s, 0, 0)),
        out_shape=jax.ShapeDtypeStruct((2, 16, pos_count, windows, SLOT), BF16),
        scratch_shapes=[
            pltpu.VMEM((2 * SLOT, D), BF16),
            pltpu.VMEM((D // 128, windows * pairs, 128), F32),
            pltpu.SemaphoreType.DMA((6,)),
        ],
        compiler_params=pltpu.CompilerParams(vmem_limit_bytes=48 * 1024 * 1024),
        cost_estimate=pl.CostEstimate(flops=2 * 1024 * 1024 * D, bytes_accessed=14_000_000, transcendentals=0),
    )(tokens, keep_index, norm_gain.reshape(1, D), w_qkv)


def attend_kernel(in_ref, out_ref):
    senders, groups, windows, _ = in_ref.shape
    total = senders * windows
    scale = 1.0 / math.sqrt(HEAD_DIM)
    flags = in_ref[:, 0, :, SLOT - 128:].astype(F32).reshape(total, 128)
    lane = lax.broadcasted_iota(jnp.int32, flags.shape, 1)
    flags = jnp.where(lane >= FLAG - (SLOT - 128), flags, 0.0).astype(BF16)
    same = lax.dot_general(flags, flags, (((1,), (1,)), ((), ())), preferred_element_type=F32) > 0.5
    results = []
    for g in range(groups):
        block = in_ref[:, g].astype(F32).reshape(total, SLOT).astype(BF16)
        query = block[:, :HEAD_DIM]
        key = block[:, HEAD_DIM:2 * HEAD_DIM]
        value = block[:, 2 * HEAD_DIM:3 * HEAD_DIM]
        scores = lax.dot_general(query, key, (((1,), (1,)), ((), ())), preferred_element_type=F32) * scale
        scores = jnp.where(same, scores, -jnp.inf)
        top = jnp.max(scores, axis=-1, keepdims=True)
        exponent = jnp.exp(scores - top)
        weights = exponent * (1.0 / jnp.sum(exponent, axis=-1, keepdims=True))
        results.append(jnp.dot(weights.astype(BF16), value, preferred_element_type=F32))
    attended = jnp.concatenate(results, axis=-1)
    out_ref[...] = attended.reshape(senders, windows, groups * HEAD_DIM).astype(BF16)


def attend(received):
    senders, groups, windows, _ = received.shape
    return pl.pallas_call(
        attend_kernel,
        out_shape=jax.ShapeDtypeStruct((senders, windows, groups * HEAD_DIM), BF16),
        compiler_params=pltpu.CompilerParams(vmem_limit_bytes=48 * 1024 * 1024),
        cost_estimate=pl.CostEstimate(flops=8 * 4 * 256 ** 3, bytes_accessed=2_800_000, transcendentals=8 * 65536),
    )(received)


def finish_kernel(place_ref, attended_ref, w_ref, tokens_ref, out_ref, sum_ref):
    windows = attended_ref.shape[2]
    pairs = attended_ref.shape[1]
    columns = out_ref.shape[2]
    depth = attended_ref.shape[3]
    total = None
    for head in range(2):
        rows = attended_ref[head].astype(F32).reshape(pairs * windows, depth).astype(BF16)
        term = jnp.dot(rows, w_ref[:, head].reshape(depth, columns), preferred_element_type=F32)
        total = term if total is None else total + term
    for c in range(columns // 128):
        sum_ref[c] = total[:, c * 128:(c + 1) * 128]
    for w in range(windows):
        for c in range(columns // 128):
            lanes = slice(c * 128, (c + 1) * 128)
            added = sum_ref[c, pl.ds(w, pairs, stride=windows), :]
            out_ref[w, :, lanes] = (tokens_ref[w, :, lanes].astype(F32) + added).astype(BF16)


def finish(place, attended, w_all, tokens):
    windows = tokens.shape[0]
    columns = 512
    return pl.pallas_call(
        finish_kernel,
        grid_spec=pltpu.PrefetchScalarGridSpec(
            num_scalar_prefetch=1,
            grid=(D // columns,),
            in_specs=[
                pl.BlockSpec((2, 16, windows, 8 * HEAD_DIM), lambda n, place: (0, 0, 0, 0)),
                pl.BlockSpec((8, 2, HEAD_DIM, columns), lambda n, place: (0, 0, 0, n)),
                pl.BlockSpec((windows, 16, columns), lambda n, place: (0, place[0], n)),
            ],
            out_specs=pl.BlockSpec((windows, 16, columns), lambda n, place: (0, 0, n)),
            scratch_shapes=[pltpu.VMEM((columns // 128, windows * 16, 128), F32)],
        ),
        out_shape=jax.ShapeDtypeStruct((windows, 16, D), BF16),
        compiler_params=pltpu.CompilerParams(vmem_limit_bytes=48 * 1024 * 1024),
        cost_estimate=pl.CostEstimate(flops=2 * 128 * D * D, bytes_accessed=15_000_000, transcendentals=0),
    )(place, attended, w_all, tokens)


def local(tokens, keep_index, norm_gain, w_qkv, w_out):
    windows = tokens.shape[0]
    w_all = lax.all_gather(w_out, "pos", axis=0, tiled=False)
    sent = project(tokens, keep_index, norm_gain, w_qkv)
    received = lax.all_to_all(
        sent.reshape(256, windows, SLOT), ("win", "pos"), split_axis=0, concat_axis=0, tiled=True
    )
    attended = attend(received.reshape(32, 8, windows, SLOT))
    returned = lax.all_to_all(attended, "win", split_axis=0, concat_axis=0, tiled=True)
    place = lax.axis_index("pos").astype(jnp.int32).reshape(1)
    return finish(
        place,
        returned.reshape(2, 16, windows, 8 * HEAD_DIM),
        w_all.reshape(8, 2, HEAD_DIM, D),
        tokens,
    )


def solution(mesh):
    in_specs = (P("win", None, None), P("win", None), P(), P(None, "pos", None), P("pos", None))
    out_specs = P("win", "pos", None)
    return jax.shard_map(local, mesh=mesh, in_specs=in_specs, out_specs=out_specs, check_vma=False)
```

```python
import math

import jax
import jax.numpy as jnp
from jax import lax
from jax.experimental import pallas as pl
from jax.experimental.pallas import tpu as pltpu
from jax.sharding import Mesh, PartitionSpec as P

D = 2560
HEADS = 16
HEAD_DIM = D // HEADS
GROUP = 2 * HEAD_DIM
NORM_EPSILON = 1e-05
WINDOWS = 8
PAIRS = 128
SLOT = 512
FLAG = 3 * HEAD_DIM
LAST = SLOT - 128
X_COUNT = 4
PLANE = 32

F32 = jnp.float32
BF16 = jnp.bfloat16
VMEM = pl.BlockSpec(memory_space=pltpu.VMEM)
HBM = pl.BlockSpec(memory_space=pltpu.HBM)
LIMIT = 60 * 1024 * 1024

BLOCK = 32
BLOCKS = PAIRS // BLOCK


def project_kernel(tokens_hbm, keep_hbm, gain_hbm, w_hbm, out_hbm, out_ref, gain_ref, x_ref, keep_ref, w_ref, spread_ref, *rest):
    rows_refs, sems = rest[:BLOCKS], rest[BLOCKS]
    rows = WINDOWS * BLOCK
    token_copies = [
        pltpu.make_async_copy(tokens_hbm.at[:, pl.ds(b * BLOCK, BLOCK)], x_ref.at[b], sems.at[b, 0])
        for b in range(BLOCKS)
    ]
    w_copies = [
        [
            pltpu.make_async_copy(
                w_hbm.at[c, pl.ds(h * HEAD_DIM, HEAD_DIM)],
                w_ref.at[pl.ds(h * SLOT + c * HEAD_DIM, HEAD_DIM)],
                sems.at[BLOCKS + h, c],
            )
            for c in range(3)
        ]
        for h in range(2)
    ]
    keep_copy = pltpu.make_async_copy(keep_hbm, keep_ref, sems.at[BLOCKS + 2, 0])
    gain_copy = pltpu.make_async_copy(gain_hbm, gain_ref, sems.at[BLOCKS + 2, 1])
    out_copies = [
        pltpu.make_async_copy(
            out_ref.at[pl.ds(b * BLOCK, BLOCK)], out_hbm.at[pl.ds(b * BLOCK, BLOCK)], sems.at[BLOCKS + 2, 2 + b]
        )
        for b in range(BLOCKS)
    ]
    gain_copy.start()
    for copy in [token_copies[0]] + w_copies[0]:
        copy.start()
    keep_copy.start()
    for h in range(2):
        w_ref[h * SLOT + FLAG:(h + 1) * SLOT, :] = jnp.zeros((SLOT - FLAG, D), BF16)
    gain_copy.wait()
    gain = gain_ref[...].reshape(1, D)

    def norm(b, w):
        x = x_ref[b, w].astype(F32)
        mean = jnp.sum(x, axis=-1, keepdims=True) * (1.0 / D)
        centered = x - mean
        variance = jnp.sum(centered * centered, axis=-1, keepdims=True) * (1.0 / D)
        normed = centered * lax.rsqrt(variance + NORM_EPSILON) * gain
        rows_refs[b][w * BLOCK:(w + 1) * BLOCK, :] = normed.astype(BF16)

    row = lax.broadcasted_iota(jnp.int32, (rows, WINDOWS), 0)
    pick_window = (row // BLOCK == lax.broadcasted_iota(jnp.int32, (rows, WINDOWS), 1)).astype(F32)
    lane = lax.broadcasted_iota(jnp.int32, (rows, 128), 1)
    row_pair = lax.broadcasted_iota(jnp.int32, (rows, 128), 0) % BLOCK

    token_copies[0].wait()
    for copy in w_copies[1] + [token_copies[1]]:
        copy.start()
    for w in range(WINDOWS):
        norm(0, w)
    keep_copy.wait()
    spread = jnp.dot(pick_window, (keep_ref[...] & 1).astype(F32), preferred_element_type=F32)
    for b in range(BLOCKS):
        if b + 2 < BLOCKS:
            token_copies[b + 2].start()
        odd = jnp.sum(jnp.where(row_pair + b * BLOCK == lane, spread, 0.0), axis=-1, keepdims=True)
        for h in range(2):
            if b == 0:
                for copy in w_copies[h]:
                    copy.wait()
            part = lax.dot_general(
                rows_refs[b][...],
                w_ref[h * SLOT:(h + 1) * SLOT, :],
                (((1,), (1,)), ((), ())),
                preferred_element_type=F32,
            )
            for c in range(SLOT // 128):
                lanes = slice(c * 128, (c + 1) * 128)
                piece = part[:, lanes]
                if c == LAST // 128:
                    piece = jnp.where(
                        lane == FLAG - LAST, odd, jnp.where(lane == FLAG - LAST + 1, 1.0 - odd, piece)
                    )
                at = h * (SLOT // 128) + c
                for w in range(WINDOWS):
                    spread_ref[b % 2, at, pl.ds(w, BLOCK, stride=WINDOWS), :] = piece[w * BLOCK:(w + 1) * BLOCK]
                out_ref[b * BLOCK:(b + 1) * BLOCK, h, :, lanes] = (
                    spread_ref[b % 2, at].reshape(BLOCK, WINDOWS, 128).astype(BF16)
                )
        out_copies[b].start()
        if b + 1 < BLOCKS:
            token_copies[b + 1].wait()
            for w in range(WINDOWS):
                norm(b + 1, w)
    for copy in out_copies:
        copy.wait()


def project(tokens, keep_index, norm_gain, w_qkv):
    rows = WINDOWS * BLOCK
    return pl.pallas_call(
        project_kernel,
        in_specs=[HBM, HBM, HBM, HBM],
        out_specs=HBM,
        out_shape=jax.ShapeDtypeStruct((PAIRS, 2, WINDOWS, SLOT), BF16),
        scratch_shapes=[
            pltpu.VMEM((PAIRS, 2, WINDOWS, SLOT), BF16),
            pltpu.VMEM((D,), F32),
            pltpu.VMEM((BLOCKS, WINDOWS, BLOCK, D), BF16),
            pltpu.VMEM((WINDOWS, PAIRS), jnp.int32),
            pltpu.VMEM((2 * SLOT, D), BF16),
            pltpu.VMEM((2, 2 * SLOT // 128, rows, 128), F32),
        ]
        + [pltpu.VMEM((rows, D), BF16)] * BLOCKS
        + [pltpu.SemaphoreType.DMA((BLOCKS + 3, WINDOWS))],
        compiler_params=pltpu.CompilerParams(vmem_limit_bytes=LIMIT),
        cost_estimate=pl.CostEstimate(flops=2 * 1024 * 1024 * D, bytes_accessed=14_000_000, transcendentals=0),
    )(tokens, keep_index, norm_gain, w_qkv)


def attend_kernel(in_ref, out_ref):
    total = PLANE * WINDOWS
    scale = 1.0 / math.sqrt(HEAD_DIM)
    flags = in_ref[0, :, 0, :, LAST:].astype(F32).reshape(total, 128)
    lane = lax.broadcasted_iota(jnp.int32, flags.shape, 1)
    flags = jnp.where(lane >= FLAG - LAST, flags, 0.0).astype(BF16)
    same = lax.dot_general(flags, flags, (((1,), (1,)), ((), ())), preferred_element_type=F32) > 0.5
    me = lax.axis_index("x")
    heads, tails = [], []
    for d in range(X_COUNT):
        source = lax.rem(me - d + X_COUNT, X_COUNT)
        group = []
        for h in range(2):
            block = in_ref[source, :, h].astype(F32).reshape(total, SLOT).astype(BF16)
            query = block[:, :HEAD_DIM]
            key = block[:, HEAD_DIM:2 * HEAD_DIM]
            value = block[:, 2 * HEAD_DIM:3 * HEAD_DIM]
            scores = lax.dot_general(query, key, (((1,), (1,)), ((), ())), preferred_element_type=F32) * scale
            scores = jnp.where(same, scores, -jnp.inf)
            top = jnp.max(scores, axis=-1, keepdims=True)
            exponent = jnp.exp(scores - top)
            weights = exponent * (1.0 / jnp.sum(exponent, axis=-1, keepdims=True))
            group.append(jnp.dot(weights.astype(BF16), value, preferred_element_type=F32))
        group = jnp.concatenate(group, axis=-1)
        heads.append(group[:, :256])
        tails.append(group[:, 256:])
    attended = jnp.concatenate(heads + tails, axis=-1)
    out_ref[...] = attended.reshape(PLANE, WINDOWS, X_COUNT * GROUP).astype(BF16)


def attend(received):
    return pl.pallas_call(
        attend_kernel,
        in_specs=[VMEM],
        out_specs=VMEM,
        out_shape=jax.ShapeDtypeStruct((PLANE, WINDOWS, X_COUNT * GROUP), BF16),
        compiler_params=pltpu.CompilerParams(vmem_limit_bytes=48 * 1024 * 1024),
        cost_estimate=pl.CostEstimate(flops=8 * 4 * 256 ** 3, bytes_accessed=2_800_000, transcendentals=8 * 65536),
    )(received)


CHUNK = 512
CHUNKS = D // CHUNK


def finish_kernel(attended_ref, w0, w1, w2a, w2b, w3, tokens_hbm, own_ref, other_ref, w_ref, t_ref, x_ref, rows_ref, sems):
    core = lax.axis_index("c")
    first = pl.multiple_of((lax.axis_index("x") * 2 + core) * 16, 16)
    token_copy = pltpu.make_async_copy(tokens_hbm.at[:, pl.ds(first, 16)], t_ref, sems.at[CHUNKS, 0])
    parts = []
    for d, w in ((0, w0), (1, w1), (3, w3)):
        parts += [(w, 0, 256, d * 256), (w, 256, 64, 1024 + d * 64)]
    parts += [(w2a, 0, 160, 512), (w2b, 0, 96, 672), (w2b, 96, 64, 1152)]
    copies = [
        [
            pltpu.make_async_copy(
                w.at[pl.ds(lo, size), pl.ds(n * CHUNK, CHUNK)],
                w_ref.at[pl.ds(to, size), pl.ds(n * CHUNK, CHUNK)],
                sems.at[n, i],
            )
            for i, (w, lo, size, to) in enumerate(parts)
        ]
        for n in range(CHUNKS)
    ]
    for copy in copies[0]:
        copy.start()
    token_copy.start()
    for n in range(1, CHUNKS):
        for copy in copies[n]:
            copy.start()
    for c in range(X_COUNT * GROUP // 128):
        lanes = slice(c * 128, (c + 1) * 128)
        x_ref[c] = attended_ref[:, :, lanes].astype(F32).reshape(PLANE * WINDOWS, 128)
        for half, start in ((0, core * 128), (1, (1 - core) * 128)):
            for w in range(WINDOWS):
                to = half * 128 + w * 16
                rows_ref[to:to + 16, lanes] = x_ref[c, pl.ds(start + w, 16, stride=WINDOWS), :].astype(BF16)
    for n in range(CHUNKS):
        lanes = slice(n * CHUNK, (n + 1) * CHUNK)
        for copy in copies[n]:
            copy.wait()
        total = jnp.dot(rows_ref[...], w_ref[:, lanes], preferred_element_type=F32)
        if n == 0:
            token_copy.wait()
        own_ref[:, :, lanes] = t_ref[:, :, lanes].astype(F32) + total[:128].reshape(WINDOWS, 16, CHUNK)
        other_ref[:, :, lanes] = total[128:].reshape(WINDOWS, 16, CHUNK).astype(BF16)


def finish(attended, weights, tokens):
    return pl.pallas_call(
        finish_kernel,
        in_specs=[VMEM] + [HBM] * 6,
        out_specs=(VMEM, VMEM),
        out_shape=(
            jax.ShapeDtypeStruct((WINDOWS, 16, D), F32),
            jax.ShapeDtypeStruct((WINDOWS, 16, D), BF16),
        ),
        scratch_shapes=[
            pltpu.VMEM((X_COUNT * GROUP, D), BF16),
            pltpu.VMEM((WINDOWS, 16, D), BF16),
            pltpu.VMEM((X_COUNT * GROUP // 128, PLANE * WINDOWS, 128), F32),
            pltpu.VMEM((PLANE * WINDOWS, X_COUNT * GROUP), BF16),
            pltpu.SemaphoreType.DMA((CHUNKS + 1, 9)),
        ],
        compiler_params=pltpu.CompilerParams(vmem_limit_bytes=50 * 1024 * 1024),
        cost_estimate=pl.CostEstimate(flops=2 * 256 * 1280 * D, bytes_accessed=9_000_000, transcendentals=0),
    )(attended, *weights, tokens)


def shift(value, axis, by):
    count = lax.axis_size(axis)
    return lax.ppermute(value, axis, [(i, (i + by) % count) for i in range(count)])


def local(tokens, keep_index, norm_gain, w_qkv, w_out):
    w1 = shift(w_out, "x", 1)
    w3 = shift(w_out, "x", -1)
    w2a = shift(w1[:HEAD_DIM], "x", 1)
    w2b = shift(w3[HEAD_DIM:], "x", -1)
    sent = project(tokens, keep_index, norm_gain, w_qkv)
    received = lax.all_to_all(
        sent.reshape(X_COUNT * PLANE, 2 * WINDOWS, SLOT), ("x", "y", "z"), split_axis=0, concat_axis=0, tiled=True
    )
    attended = attend(received.reshape(X_COUNT, PLANE, 2, WINDOWS, SLOT))
    returned = lax.all_to_all(attended, ("y", "z"), split_axis=0, concat_axis=0, tiled=True)
    own, other = finish(returned, (w_out, w1, w2a, w2b, w3), tokens)
    return (own + shift(other, "c", 1).astype(F32)).astype(BF16)


def solution(mesh):
    mesh = Mesh(mesh.devices.reshape(4, 8, 4, 2), ("y", "z", "x", "c"))
    win, pos = ("y", "z"), ("x", "c")
    in_specs = (P(win, None, None), P(win, None), P(), P(None, pos, None), P(pos, None))
    return jax.shard_map(local, mesh=mesh, in_specs=in_specs, out_specs=P(win, pos, None), check_vma=False)
```

```python
import math

import jax
import jax.numpy as jnp
from jax import lax
from jax.experimental import pallas as pl
from jax.experimental.pallas import tpu as pltpu
from jax.sharding import Mesh, PartitionSpec as P

D = 2560
HEADS = 16
HEAD_DIM = D // HEADS
GROUP = 2 * HEAD_DIM
NORM_EPSILON = 1e-05
WINDOWS = 8
PAIRS = 128
SLOT = 512
LAST = SLOT - 128
TAIL = HEAD_DIM - 128
FLAG = 3 * TAIL
X_COUNT = 4
PLANE = 32

F32 = jnp.float32
BF16 = jnp.bfloat16
VMEM = pl.BlockSpec(memory_space=pltpu.VMEM)
HBM = pl.BlockSpec(memory_space=pltpu.HBM)
LIMIT = 60 * 1024 * 1024

BLOCK = 32
BLOCKS = PAIRS // BLOCK


def project_kernel(tokens_hbm, keep_hbm, gain_hbm, w_hbm, out_hbm, out_ref, gain_ref, x_ref, keep_ref, w_ref, spread_ref, *rest):
    rows_refs, sems = rest[:BLOCKS], rest[BLOCKS]
    rows = WINDOWS * BLOCK
    token_copies = [
        pltpu.make_async_copy(tokens_hbm.at[:, pl.ds(b * BLOCK, BLOCK)], x_ref.at[b], sems.at[b, 0])
        for b in range(BLOCKS)
    ]
    w_copies = [
        [pltpu.make_async_copy(w_hbm.at[:, h, pl.ds(0, 128)], w_ref.at[h, pl.ds(0, 3)], sems.at[BLOCKS + h, 3])]
        + [
            pltpu.make_async_copy(
                w_hbm.at[c, h, pl.ds(128, TAIL)], w_ref.at[h, 3, pl.ds(c * TAIL, TAIL)], sems.at[BLOCKS + h, c]
            )
            for c in range(3)
        ]
        for h in range(2)
    ]
    keep_copy = pltpu.make_async_copy(keep_hbm, keep_ref, sems.at[BLOCKS + 2, 0])
    gain_copy = pltpu.make_async_copy(gain_hbm, gain_ref, sems.at[BLOCKS + 2, 1])
    out_copies = [
        pltpu.make_async_copy(
            out_ref.at[pl.ds(b * BLOCK, BLOCK)], out_hbm.at[pl.ds(b * BLOCK, BLOCK)], sems.at[BLOCKS + 2, 2 + b]
        )
        for b in range(BLOCKS)
    ]
    gain_copy.start()
    for copy in [token_copies[0]] + w_copies[0]:
        copy.start()
    keep_copy.start()
    for h in range(2):
        w_ref[h, 3, FLAG:, :] = jnp.zeros((128 - FLAG, D), BF16)
    gain_copy.wait()
    gain = gain_ref[...].reshape(1, D)

    def norm(b, w):
        x = x_ref[b, w].astype(F32)
        mean = jnp.sum(x, axis=-1, keepdims=True) * (1.0 / D)
        centered = x - mean
        variance = jnp.sum(centered * centered, axis=-1, keepdims=True) * (1.0 / D)
        normed = centered * lax.rsqrt(variance + NORM_EPSILON) * gain
        rows_refs[b][w * BLOCK:(w + 1) * BLOCK, :] = normed.astype(BF16)

    row = lax.broadcasted_iota(jnp.int32, (rows, WINDOWS), 0)
    pick_window = (row // BLOCK == lax.broadcasted_iota(jnp.int32, (rows, WINDOWS), 1)).astype(F32)
    lane = lax.broadcasted_iota(jnp.int32, (rows, 128), 1)
    row_pair = lax.broadcasted_iota(jnp.int32, (rows, 128), 0) % BLOCK

    token_copies[0].wait()
    for copy in w_copies[1] + [token_copies[1]]:
        copy.start()
    for w in range(WINDOWS):
        norm(0, w)
    keep_copy.wait()
    spread = jnp.dot(pick_window, (keep_ref[...] & 1).astype(F32), preferred_element_type=F32)
    for b in range(BLOCKS):
        if b + 2 < BLOCKS:
            token_copies[b + 2].start()
        odd = jnp.sum(jnp.where(row_pair + b * BLOCK == lane, spread, 0.0), axis=-1, keepdims=True)
        for h in range(2):
            if b == 0:
                for copy in w_copies[h]:
                    copy.wait()
            part = lax.dot_general(
                rows_refs[b][...],
                w_ref[h].reshape(SLOT, D),
                (((1,), (1,)), ((), ())),
                preferred_element_type=F32,
            )
            for c in range(SLOT // 128):
                lanes = slice(c * 128, (c + 1) * 128)
                piece = part[:, lanes]
                if c == LAST // 128:
                    piece = jnp.where(
                        lane == FLAG, odd, jnp.where(lane == FLAG + 1, 1.0 - odd, piece)
                    )
                at = h * (SLOT // 128) + c
                for w in range(WINDOWS):
                    spread_ref[b % 2, at, pl.ds(w, BLOCK, stride=WINDOWS), :] = piece[w * BLOCK:(w + 1) * BLOCK]
                out_ref[b * BLOCK:(b + 1) * BLOCK, h, :, lanes] = (
                    spread_ref[b % 2, at].reshape(BLOCK, WINDOWS, 128).astype(BF16)
                )
        out_copies[b].start()
        if b + 1 < BLOCKS:
            token_copies[b + 1].wait()
            for w in range(WINDOWS):
                norm(b + 1, w)
    for copy in out_copies:
        copy.wait()


def project(tokens, keep_index, norm_gain, w_qkv):
    rows = WINDOWS * BLOCK
    return pl.pallas_call(
        project_kernel,
        in_specs=[HBM, HBM, HBM, HBM],
        out_specs=HBM,
        out_shape=jax.ShapeDtypeStruct((PAIRS, 2, WINDOWS, SLOT), BF16),
        scratch_shapes=[
            pltpu.VMEM((PAIRS, 2, WINDOWS, SLOT), BF16),
            pltpu.VMEM((D,), F32),
            pltpu.VMEM((BLOCKS, WINDOWS, BLOCK, D), BF16),
            pltpu.VMEM((WINDOWS, PAIRS), jnp.int32),
            pltpu.VMEM((2, 4, 128, D), BF16),
            pltpu.VMEM((2, 2 * SLOT // 128, rows, 128), F32),
        ]
        + [pltpu.VMEM((rows, D), BF16)] * BLOCKS
        + [pltpu.SemaphoreType.DMA((BLOCKS + 3, WINDOWS))],
        compiler_params=pltpu.CompilerParams(vmem_limit_bytes=LIMIT),
        cost_estimate=pl.CostEstimate(flops=2 * 1024 * 1024 * D, bytes_accessed=14_000_000, transcendentals=0),
    )(tokens, keep_index, norm_gain, w_qkv.reshape(3, 2, HEAD_DIM, D))


BATCH = 4


def attend_kernel(in_ref, out_ref):
    total = PLANE * WINDOWS
    scale = 1.0 / math.sqrt(HEAD_DIM)
    lane = lax.broadcasted_iota(jnp.int32, (total, 128), 1)
    flags = in_ref[0, :, 0, :, LAST:].astype(F32).reshape(total, 128)
    flags = jnp.where(lane >= FLAG, flags, 0.0).astype(BF16)
    same = lax.dot_general(flags, flags, (((1,), (1,)), ((), ())), preferred_element_type=F32) > 0.5
    me = lax.axis_index("x")
    units = [(d, h) for d in range(X_COUNT) for h in range(2)]
    tails = []
    for first in range(0, 8, BATCH):
        group = units[first:first + BATCH]
        scores, values = [], []
        for d, h in group:
            source = lax.rem(me - d + X_COUNT, X_COUNT)

            def part(i):
                return in_ref[source, :, h, :, i * 128:(i + 1) * 128].astype(F32).reshape(total, 128)

            last = part(3)
            query = jnp.concatenate([part(0), jnp.where(lane < TAIL, last, 0.0)], axis=-1).astype(BF16)
            key = jnp.concatenate([part(1), pltpu.roll(last, 128 - TAIL, 1)], axis=-1).astype(BF16)
            value_tail = jnp.where(lane < TAIL, pltpu.roll(last, 128 - 2 * TAIL, 1), 1.0)
            values.append(jnp.concatenate([part(2), value_tail], axis=-1).astype(BF16))
            scores.append(lax.dot_general(query, key, (((1,), (1,)), ((), ())), preferred_element_type=F32))
        weights = []
        for score in scores:
            score = jnp.where(same, score * scale, -jnp.inf)
            weights.append(jnp.exp(score - jnp.max(score, axis=-1, keepdims=True)).astype(BF16))
        mixes = [jnp.dot(w, v, preferred_element_type=F32) for w, v in zip(weights, values)]
        for (d, h), mixed in zip(group, mixes):
            unit = d * 2 + h
            scaled = mixed * (1.0 / mixed[:, 128 + TAIL:128 + TAIL + 1])
            out_ref[:, :, unit * 128:(unit + 1) * 128] = scaled[:, :128].reshape(PLANE, WINDOWS, 128).astype(BF16)
            tail = scaled[:, 128:]
            place = unit % 4
            if place == 0:
                gathered = tail
            else:
                gathered = jnp.where(lane < place * TAIL, gathered, pltpu.roll(tail, place * TAIL, 1))
            if place == 3:
                tails.append(gathered)
    for i, tail in enumerate(tails):
        at = 1024 + i * 128
        out_ref[:, :, at:at + 128] = tail.reshape(PLANE, WINDOWS, 128).astype(BF16)


def attend(received):
    return pl.pallas_call(
        attend_kernel,
        in_specs=[VMEM],
        out_specs=VMEM,
        out_shape=jax.ShapeDtypeStruct((PLANE, WINDOWS, X_COUNT * GROUP), BF16),
        compiler_params=pltpu.CompilerParams(vmem_limit_bytes=48 * 1024 * 1024),
        cost_estimate=pl.CostEstimate(flops=8 * 4 * 256 ** 3, bytes_accessed=2_800_000, transcendentals=8 * 65536),
    )(received)


CHUNK = 512
CHUNKS = D // CHUNK


def finish_kernel(attended_ref, w0, w1, w2a, w2b, w3, tokens_hbm, own_ref, other_ref, *scratch):
    w_ref, w_tail_ref, t_ref, x_ref, rows_ref, sems = scratch
    core = lax.axis_index("c")
    first = pl.multiple_of((lax.axis_index("x") * 2 + core) * 16, 16)
    token_copy = pltpu.make_async_copy(tokens_hbm.at[:, pl.ds(first, 16)], t_ref, sems.at[CHUNKS, 0])
    parts = [(w0, 0), (w1, 2), (w2a, 4), (w2b, 5), (w3, 6)]
    copies = [
        [
            pltpu.make_async_copy(
                w.at[:, pl.ds(lo, size), pl.ds(n * CHUNK, CHUNK)],
                to_ref.at[pl.ds(head, w.shape[0]), :, pl.ds(n * CHUNK, CHUNK)],
                sems.at[n, i * 2 + j],
            )
            for i, (w, head) in enumerate(parts)
            for j, (lo, size, to_ref) in enumerate(((0, 128, w_ref), (128, TAIL, w_tail_ref)))
        ]
        for n in range(CHUNKS)
    ]
    for copy in copies[0]:
        copy.start()
    token_copy.start()
    for n in range(1, CHUNKS):
        for copy in copies[n]:
            copy.start()
    for c in range(X_COUNT * GROUP // 128):
        lanes = slice(c * 128, (c + 1) * 128)
        x_ref[c] = attended_ref[:, :, lanes].astype(F32).reshape(PLANE * WINDOWS, 128)
        for half, start in ((0, core * 128), (1, (1 - core) * 128)):
            for w in range(WINDOWS):
                to = half * 128 + w * 16
                rows_ref[to:to + 16, lanes] = x_ref[c, pl.ds(start + w, 16, stride=WINDOWS), :].astype(BF16)
    for n in range(CHUNKS):
        lanes = slice(n * CHUNK, (n + 1) * CHUNK)
        for copy in copies[n]:
            copy.wait()
        total = jnp.dot(
            rows_ref[:, :1024], w_ref[:, :, lanes].reshape(1024, CHUNK), preferred_element_type=F32
        ) + jnp.dot(rows_ref[:, 1024:], w_tail_ref[:, :, lanes].reshape(256, CHUNK), preferred_element_type=F32)
        if n == 0:
            token_copy.wait()
        own_ref[:, :, lanes] = t_ref[:, :, lanes].astype(F32) + total[:128].reshape(WINDOWS, 16, CHUNK)
        other_ref[:, :, lanes] = total[128:].reshape(WINDOWS, 16, CHUNK).astype(BF16)


def finish(attended, weights, tokens):
    return pl.pallas_call(
        finish_kernel,
        in_specs=[VMEM] + [HBM] * 6,
        out_specs=(VMEM, VMEM),
        out_shape=(
            jax.ShapeDtypeStruct((WINDOWS, 16, D), F32),
            jax.ShapeDtypeStruct((WINDOWS, 16, D), BF16),
        ),
        scratch_shapes=[
            pltpu.VMEM((8, 128, D), BF16),
            pltpu.VMEM((8, TAIL, D), BF16),
            pltpu.VMEM((WINDOWS, 16, D), BF16),
            pltpu.VMEM((X_COUNT * GROUP // 128, PLANE * WINDOWS, 128), F32),
            pltpu.VMEM((PLANE * WINDOWS, X_COUNT * GROUP), BF16),
            pltpu.SemaphoreType.DMA((CHUNKS + 1, 10)),
        ],
        compiler_params=pltpu.CompilerParams(vmem_limit_bytes=50 * 1024 * 1024),
        cost_estimate=pl.CostEstimate(flops=2 * 256 * 1280 * D, bytes_accessed=9_000_000, transcendentals=0),
    )(attended, *[w.reshape(-1, HEAD_DIM, D) for w in weights], tokens)


def shift(value, axis, by):
    count = lax.axis_size(axis)
    return lax.ppermute(value, axis, [(i, (i + by) % count) for i in range(count)])


def local(tokens, keep_index, norm_gain, w_qkv, w_out):
    w1 = shift(w_out, "x", 1)
    w3 = shift(w_out, "x", -1)
    w2a = shift(w1[:HEAD_DIM], "x", 1)
    w2b = shift(w3[HEAD_DIM:], "x", -1)
    sent = project(tokens, keep_index, norm_gain, w_qkv)
    received = lax.all_to_all(
        sent.reshape(X_COUNT * PLANE, 2 * WINDOWS, SLOT), ("x", "y", "z"), split_axis=0, concat_axis=0, tiled=True
    )
    attended = attend(received.reshape(X_COUNT, PLANE, 2, WINDOWS, SLOT))
    returned = lax.all_to_all(attended, ("y", "z"), split_axis=0, concat_axis=0, tiled=True)
    own, other = finish(returned, (w_out, w1, w2a, w2b, w3), tokens)
    return (own + shift(other, "c", 1).astype(F32)).astype(BF16)


def solution(mesh):
    mesh = Mesh(mesh.devices.reshape(4, 8, 4, 2), ("y", "z", "x", "c"))
    win, pos = ("y", "z"), ("x", "c")
    in_specs = (P(win, None, None), P(win, None), P(), P(None, pos, None), P(pos, None))
    return jax.shard_map(local, mesh=mesh, in_specs=in_specs, out_specs=P(win, pos, None), check_vma=False)
```

```python
import math

import jax
import jax.numpy as jnp
from jax import lax
from jax.experimental import pallas as pl
from jax.experimental.pallas import tpu as pltpu
from jax.sharding import Mesh, PartitionSpec as P

D = 2560
HEADS = 16
HEAD_DIM = D // HEADS
GROUP = 2 * HEAD_DIM
NORM_EPSILON = 1e-05
WINDOWS = 8
PAIRS = 128
SLOT = 512
LAST = SLOT - 128
TAIL = HEAD_DIM - 128
FLAG = 3 * TAIL
X_COUNT = 4
PLANE = 32

F32 = jnp.float32
BF16 = jnp.bfloat16
VMEM = pl.BlockSpec(memory_space=pltpu.VMEM)
HBM = pl.BlockSpec(memory_space=pltpu.HBM)
LIMIT = 60 * 1024 * 1024

BLOCK = 32
BLOCKS = PAIRS // BLOCK


def project_kernel(tokens_hbm, keep_hbm, gain_hbm, w_hbm, out_hbm, out_ref, gain_ref, x_ref, keep_ref, w_ref, *rest):
    rows_refs, sems = rest[:BLOCKS], rest[BLOCKS]
    rows = WINDOWS * BLOCK
    token_copies = [
        pltpu.make_async_copy(tokens_hbm.at[:, pl.ds(b * BLOCK, BLOCK)], x_ref.at[b], sems.at[b, 0])
        for b in range(BLOCKS)
    ]
    w_copies = [
        [pltpu.make_async_copy(w_hbm.at[:, h, pl.ds(0, 128)], w_ref.at[h, pl.ds(0, 3)], sems.at[BLOCKS + h, 3])]
        + [
            pltpu.make_async_copy(
                w_hbm.at[c, h, pl.ds(128, TAIL)], w_ref.at[h, 3, pl.ds(c * TAIL, TAIL)], sems.at[BLOCKS + h, c]
            )
            for c in range(3)
        ]
        for h in range(2)
    ]
    keep_copy = pltpu.make_async_copy(keep_hbm, keep_ref, sems.at[BLOCKS + 2, 0])
    gain_copy = pltpu.make_async_copy(gain_hbm, gain_ref, sems.at[BLOCKS + 2, 1])
    out_copies = [
        [
            pltpu.make_async_copy(
                out_ref.at[pl.ds(b * BLOCK, BLOCK), h], out_hbm.at[pl.ds(b * BLOCK, BLOCK), h], sems.at[b, 1 + h]
            )
            for h in range(2)
        ]
        for b in range(BLOCKS)
    ]
    gain_copy.start()
    for copy in [token_copies[0]] + w_copies[0]:
        copy.start()
    keep_copy.start()
    for h in range(2):
        w_ref[h, 3, FLAG:, :] = jnp.zeros((128 - FLAG, D), BF16)
    gain_copy.wait()
    gain = gain_ref[...].reshape(1, D)

    def norm(b, w):
        x = x_ref[b, w].astype(F32)
        mean = jnp.sum(x, axis=-1, keepdims=True) * (1.0 / D)
        centered = x - mean
        variance = jnp.sum(centered * centered, axis=-1, keepdims=True) * (1.0 / D)
        normed = centered * lax.rsqrt(variance + NORM_EPSILON) * gain
        rows_refs[b][w * BLOCK:(w + 1) * BLOCK, :] = normed.astype(BF16)

    row = lax.broadcasted_iota(jnp.int32, (rows, WINDOWS), 0)
    pick_window = (row // BLOCK == lax.broadcasted_iota(jnp.int32, (rows, WINDOWS), 1)).astype(F32)
    lane = lax.broadcasted_iota(jnp.int32, (rows, 128), 1)
    row_pair = lax.broadcasted_iota(jnp.int32, (rows, 128), 0) % BLOCK

    token_copies[0].wait()
    for copy in w_copies[1] + [token_copies[1]]:
        copy.start()
    for w in range(WINDOWS):
        norm(0, w)
    keep_copy.wait()
    spread = jnp.dot(pick_window, (keep_ref[...] & 1).astype(F32), preferred_element_type=F32)
    for b in range(BLOCKS):
        if b + 2 < BLOCKS:
            token_copies[b + 2].start()
        odd = jnp.sum(jnp.where(row_pair + b * BLOCK == lane, spread, 0.0), axis=-1, keepdims=True)
        for h in range(2):
            if h == 1 and b + 1 < BLOCKS:
                token_copies[b + 1].wait()
                for w in range(WINDOWS):
                    norm(b + 1, w)
            if b == 0:
                for copy in w_copies[h]:
                    copy.wait()
            part = lax.dot_general(
                rows_refs[b][...],
                w_ref[h].reshape(SLOT, D),
                (((1,), (1,)), ((), ())),
                preferred_element_type=F32,
            )
            for c in range(SLOT // 128):
                lanes = slice(c * 128, (c + 1) * 128)
                piece = part[:, lanes]
                if c == LAST // 128:
                    piece = jnp.where(
                        lane == FLAG, odd, jnp.where(lane == FLAG + 1, 1.0 - odd, piece)
                    )
                out_ref[b * BLOCK:(b + 1) * BLOCK, h, :, lanes] = jnp.swapaxes(
                    piece.reshape(WINDOWS, BLOCK, 128), 0, 1
                ).astype(BF16)
            out_copies[b][h].start()
    for copies in out_copies:
        for copy in copies:
            copy.wait()


def project(tokens, keep_index, norm_gain, w_qkv):
    rows = WINDOWS * BLOCK
    return pl.pallas_call(
        project_kernel,
        in_specs=[HBM, HBM, HBM, HBM],
        out_specs=HBM,
        out_shape=jax.ShapeDtypeStruct((PAIRS, 2, WINDOWS, SLOT), BF16),
        scratch_shapes=[
            pltpu.VMEM((PAIRS, 2, WINDOWS, SLOT), BF16),
            pltpu.VMEM((D,), F32),
            pltpu.VMEM((BLOCKS, WINDOWS, BLOCK, D), BF16),
            pltpu.VMEM((WINDOWS, PAIRS), jnp.int32),
            pltpu.VMEM((2, 4, 128, D), BF16),
        ]
        + [pltpu.VMEM((rows, D), BF16)] * BLOCKS
        + [pltpu.SemaphoreType.DMA((BLOCKS + 3, WINDOWS))],
        compiler_params=pltpu.CompilerParams(vmem_limit_bytes=LIMIT),
        cost_estimate=pl.CostEstimate(flops=2 * 1024 * 1024 * D, bytes_accessed=14_000_000, transcendentals=0),
    )(tokens, keep_index, norm_gain, w_qkv.reshape(3, 2, HEAD_DIM, D))


BATCH = 4


def attend_kernel(in_ref, out_ref):
    total = PLANE * WINDOWS
    scale = 1.0 / math.sqrt(HEAD_DIM)
    lane = lax.broadcasted_iota(jnp.int32, (total, 128), 1)
    flags = in_ref[0, :, 0, :, LAST:].astype(F32).reshape(total, 128)
    flags = jnp.where(lane >= FLAG, flags, 0.0).astype(BF16)
    same = lax.dot_general(flags, flags, (((1,), (1,)), ((), ())), preferred_element_type=F32) > 0.5
    me = lax.axis_index("x")

    def store(tile, rows):
        rows = rows.reshape(4, 8, WINDOWS, 128).astype(BF16)
        for y in range(4):
            out_ref[:, y, :, tile * 128:(tile + 1) * 128] = rows[y]

    units = [(d, h) for d in range(X_COUNT) for h in range(2)]
    tails = []
    for first in range(0, 8, BATCH):
        group = units[first:first + BATCH]
        scores, values = [], []
        for d, h in group:
            source = lax.rem(me - d + X_COUNT, X_COUNT)

            def part(i):
                return in_ref[source, :, h, :, i * 128:(i + 1) * 128].astype(F32).reshape(total, 128)

            last = part(3)
            query = jnp.concatenate([part(0), jnp.where(lane < TAIL, last, 0.0)], axis=-1).astype(BF16)
            key = jnp.concatenate([part(1), pltpu.roll(last, 128 - TAIL, 1)], axis=-1).astype(BF16)
            value_tail = jnp.where(lane < TAIL, pltpu.roll(last, 128 - 2 * TAIL, 1), 1.0)
            values.append(jnp.concatenate([part(2), value_tail], axis=-1).astype(BF16))
            scores.append(lax.dot_general(query, key, (((1,), (1,)), ((), ())), preferred_element_type=F32))
        weights = []
        for score in scores:
            score = jnp.where(same, score * scale, -jnp.inf)
            weights.append(jnp.exp(score - jnp.max(score, axis=-1, keepdims=True)).astype(BF16))
        mixes = [jnp.dot(w, v, preferred_element_type=F32) for w, v in zip(weights, values)]
        for (d, h), mixed in zip(group, mixes):
            unit = d * 2 + h
            scaled = mixed * (1.0 / mixed[:, 128 + TAIL:128 + TAIL + 1])
            store(unit, scaled[:, :128])
            tail = scaled[:, 128:]
            place = unit % 4
            if place == 0:
                gathered = tail
            else:
                gathered = jnp.where(lane < place * TAIL, gathered, pltpu.roll(tail, place * TAIL, 1))
            if place == 3:
                tails.append(gathered)
    for i, tail in enumerate(tails):
        store(8 + i, tail)


def attend(received):
    return pl.pallas_call(
        attend_kernel,
        in_specs=[VMEM],
        out_specs=VMEM,
        out_shape=jax.ShapeDtypeStruct((8, 4, WINDOWS, X_COUNT * GROUP), BF16),
        compiler_params=pltpu.CompilerParams(vmem_limit_bytes=48 * 1024 * 1024),
        cost_estimate=pl.CostEstimate(flops=8 * 4 * 256 ** 3, bytes_accessed=2_800_000, transcendentals=8 * 65536),
    )(received)


CHUNK = 512
CHUNKS = D // CHUNK


def finish_kernel(attended_ref, w0, w1, w2a, w2b, w3, tokens_hbm, own_hbm, other_hbm, *scratch):
    w_ref, w_tail_ref, t_ref, x_ref, rows_ref, own_ref, other_ref, sems, out_sems = scratch
    core = lax.axis_index("c")
    first = pl.multiple_of((lax.axis_index("x") * 2 + core) * 16, 16)
    token_copy = pltpu.make_async_copy(tokens_hbm.at[:, pl.ds(first, 16)], t_ref, sems.at[CHUNKS, 0])
    parts = [(w0, 0), (w1, 2), (w2a, 4), (w2b, 5), (w3, 6)]
    copies = [
        [
            pltpu.make_async_copy(
                w.at[:, pl.ds(lo, size), pl.ds(n * CHUNK, CHUNK)],
                to_ref.at[pl.ds(head, w.shape[0]), :, pl.ds(n * CHUNK, CHUNK)],
                sems.at[n, i * 2 + j],
            )
            for i, (w, head) in enumerate(parts)
            for j, (lo, size, to_ref) in enumerate(((0, 128, w_ref), (128, TAIL, w_tail_ref)))
        ]
        for n in range(CHUNKS)
    ]
    for copy in copies[0]:
        copy.start()
    token_copy.start()
    for n in range(1, CHUNKS):
        for copy in copies[n]:
            copy.start()
    for c in range(X_COUNT * GROUP // 128):
        lanes = slice(c * 128, (c + 1) * 128)
        x_ref[c] = attended_ref[:, :, lanes].astype(F32).reshape(PLANE * WINDOWS, 128)
        for half, owner in ((0, core), (1, 1 - core)):
            for w in range(WINDOWS):
                to = half * 128 + w * 16
                picked = [
                    x_ref[c, pl.ds((owner * 2 + y) * WINDOWS + w, 8, stride=4 * WINDOWS), :] for y in range(2)
                ]
                rows_ref[to:to + 16, lanes] = jnp.concatenate(picked, axis=0).astype(BF16)
    out_copies = []
    for n in range(CHUNKS):
        lanes = slice(n * CHUNK, (n + 1) * CHUNK)
        for copy in copies[n]:
            copy.wait()
        total = jnp.dot(
            rows_ref[:, :1024], w_ref[:, :, lanes].reshape(1024, CHUNK), preferred_element_type=F32
        ) + jnp.dot(rows_ref[:, 1024:], w_tail_ref[:, :, lanes].reshape(256, CHUNK), preferred_element_type=F32)
        if n == 0:
            token_copy.wait()
        own = t_ref[:, :, lanes].astype(F32) + total[:128].reshape(WINDOWS, 16, CHUNK)
        own_ref[:, :, lanes] = own.astype(BF16)
        other_ref[:, :, lanes] = total[128:].reshape(WINDOWS, 16, CHUNK).astype(BF16)
        columns = pl.ds(n * CHUNK, CHUNK)
        for i, (ref, hbm) in enumerate(((own_ref, own_hbm), (other_ref, other_hbm))):
            out_copies.append(
                pltpu.make_async_copy(ref.at[:, :, columns], hbm.at[:, :, columns], out_sems.at[n, i])
            )
            out_copies[-1].start()
    for copy in out_copies:
        copy.wait()


def finish(attended, weights, tokens):
    return pl.pallas_call(
        finish_kernel,
        in_specs=[VMEM] + [HBM] * 6,
        out_specs=(HBM, HBM),
        out_shape=(
            jax.ShapeDtypeStruct((WINDOWS, 16, D), BF16),
            jax.ShapeDtypeStruct((WINDOWS, 16, D), BF16),
        ),
        scratch_shapes=[
            pltpu.VMEM((8, 128, D), BF16),
            pltpu.VMEM((8, TAIL, D), BF16),
            pltpu.VMEM((WINDOWS, 16, D), BF16),
            pltpu.VMEM((X_COUNT * GROUP // 128, PLANE * WINDOWS, 128), F32),
            pltpu.VMEM((PLANE * WINDOWS, X_COUNT * GROUP), BF16),
            pltpu.VMEM((WINDOWS, 16, D), BF16),
            pltpu.VMEM((WINDOWS, 16, D), BF16),
            pltpu.SemaphoreType.DMA((CHUNKS + 1, 10)),
            pltpu.SemaphoreType.DMA((CHUNKS, 2)),
        ],
        compiler_params=pltpu.CompilerParams(vmem_limit_bytes=50 * 1024 * 1024),
        cost_estimate=pl.CostEstimate(flops=2 * 256 * 1280 * D, bytes_accessed=9_000_000, transcendentals=0),
    )(attended, *[w.reshape(-1, HEAD_DIM, D) for w in weights], tokens)


def shift(value, axis, by):
    count = lax.axis_size(axis)
    return lax.ppermute(value, axis, [(i, (i + by) % count) for i in range(count)])


def local(tokens, keep_index, norm_gain, w_qkv, w_out):
    w1 = shift(w_out, "x", 1)
    w3 = shift(w_out, "x", -1)
    w2a = shift(w1[:HEAD_DIM], "x", 1)
    w2b = shift(w3[HEAD_DIM:], "x", -1)
    sent = project(tokens, keep_index, norm_gain, w_qkv)
    received = lax.all_to_all(
        sent.reshape(X_COUNT * PLANE, 2 * WINDOWS, SLOT), ("x", "y", "z"), split_axis=0, concat_axis=0, tiled=True
    )
    attended = attend(received.reshape(X_COUNT, PLANE, 2, WINDOWS, SLOT))
    returned = lax.all_to_all(
        attended.reshape(PLANE, WINDOWS, X_COUNT * GROUP), ("z", "y"), split_axis=0, concat_axis=0, tiled=True
    )
    own, other = finish(returned, (w_out, w1, w2a, w2b, w3), tokens)
    return (own.astype(F32) + shift(other, "c", 1).astype(F32)).astype(BF16)


def solution(mesh):
    mesh = Mesh(mesh.devices.reshape(4, 8, 4, 2), ("y", "z", "x", "c"))
    win, pos = ("y", "z"), ("x", "c")
    in_specs = (P(win, None, None), P(win, None), P(), P(None, pos, None), P(pos, None))
    return jax.shard_map(local, mesh=mesh, in_specs=in_specs, out_specs=P(win, pos, None), check_vma=False)
```

```python
import math

import jax
import jax.numpy as jnp
from jax import lax
from jax.experimental import pallas as pl
from jax.experimental.pallas import tpu as pltpu
from jax.sharding import Mesh, PartitionSpec as P

D = 2560
HEADS = 16
HEAD_DIM = D // HEADS
GROUP = 2 * HEAD_DIM
NORM_EPSILON = 1e-05
WINDOWS = 8
PAIRS = 128
SLOT = 512
LAST = SLOT - 128
TAIL = HEAD_DIM - 128
FLAG = 3 * TAIL
X_COUNT = 4
PLANE = 32

F32 = jnp.float32
BF16 = jnp.bfloat16
VMEM = pl.BlockSpec(memory_space=pltpu.VMEM)
HBM = pl.BlockSpec(memory_space=pltpu.HBM)
LIMIT = 60 * 1024 * 1024

BLOCK = 32
BLOCKS = PAIRS // BLOCK


def project_kernel(tokens_hbm, keep_hbm, gain_hbm, w_hbm, out_hbm, out_ref, gain_ref, x_ref, keep_ref, w_ref, *rest):
    rows_refs, sems = rest[:BLOCKS], rest[BLOCKS]
    rows = WINDOWS * BLOCK
    token_copies = [
        pltpu.make_async_copy(tokens_hbm.at[:, pl.ds(b * BLOCK, BLOCK)], x_ref.at[b], sems.at[b, 0])
        for b in range(BLOCKS)
    ]
    w_copies = [
        [pltpu.make_async_copy(w_hbm.at[:, h, pl.ds(0, 128)], w_ref.at[h, pl.ds(0, 3)], sems.at[BLOCKS + h, 3])]
        + [
            pltpu.make_async_copy(
                w_hbm.at[c, h, pl.ds(128, TAIL)], w_ref.at[h, 3, pl.ds(c * TAIL, TAIL)], sems.at[BLOCKS + h, c]
            )
            for c in range(3)
        ]
        for h in range(2)
    ]
    keep_copy = pltpu.make_async_copy(keep_hbm, keep_ref, sems.at[BLOCKS + 2, 0])
    gain_copy = pltpu.make_async_copy(gain_hbm, gain_ref, sems.at[BLOCKS + 2, 1])
    out_copies = [
        [
            pltpu.make_async_copy(
                out_ref.at[:, b, h], out_hbm.at[:, b, h], sems.at[b, 1 + h]
            )
            for h in range(2)
        ]
        for b in range(BLOCKS)
    ]
    gain_copy.start()
    for copy in [token_copies[0]] + w_copies[0]:
        copy.start()
    keep_copy.start()
    for h in range(2):
        w_ref[h, 3, FLAG:, :] = jnp.zeros((128 - FLAG, D), BF16)
    gain_copy.wait()
    gain = gain_ref[...].reshape(1, D)

    def norm(b, w):
        x = x_ref[b, w].astype(F32)
        mean = jnp.sum(x, axis=-1, keepdims=True) * (1.0 / D)
        centered = x - mean
        variance = jnp.sum(centered * centered, axis=-1, keepdims=True) * (1.0 / D)
        normed = centered * lax.rsqrt(variance + NORM_EPSILON) * gain
        rows_refs[b][w * BLOCK:(w + 1) * BLOCK, :] = normed.astype(BF16)

    row = lax.broadcasted_iota(jnp.int32, (rows, WINDOWS), 0)
    pick_window = (row // BLOCK == lax.broadcasted_iota(jnp.int32, (rows, WINDOWS), 1)).astype(F32)
    lane = lax.broadcasted_iota(jnp.int32, (rows, 128), 1)
    row_pair = lax.broadcasted_iota(jnp.int32, (rows, 128), 0) % BLOCK

    token_copies[0].wait()
    for copy in w_copies[1] + [token_copies[1]]:
        copy.start()
    for w in range(WINDOWS):
        norm(0, w)
    keep_copy.wait()
    spread = jnp.dot(pick_window, (keep_ref[...] & 1).astype(F32), preferred_element_type=F32)
    for b in range(BLOCKS):
        if b + 2 < BLOCKS:
            token_copies[b + 2].start()
        odd = jnp.sum(jnp.where(row_pair + b * BLOCK == lane, spread, 0.0), axis=-1, keepdims=True)
        for h in range(2):
            if h == 1 and b + 1 < BLOCKS:
                token_copies[b + 1].wait()
                for w in range(WINDOWS):
                    norm(b + 1, w)
            if b == 0:
                for copy in w_copies[h]:
                    copy.wait()
            part = lax.dot_general(
                rows_refs[b][...],
                w_ref[h].reshape(SLOT, D),
                (((1,), (1,)), ((), ())),
                preferred_element_type=F32,
            )
            for c in range(SLOT // 128):
                lanes = slice(c * 128, (c + 1) * 128)
                piece = part[:, lanes]
                if c == LAST // 128:
                    piece = jnp.where(
                        lane == FLAG, odd, jnp.where(lane == FLAG + 1, 1.0 - odd, piece)
                    )
                out_ref[:, b, h, :, lanes] = jnp.swapaxes(
                    piece.reshape(WINDOWS, BLOCK, 128), 0, 1
                ).astype(BF16)
            out_copies[b][h].start()
    for copies in out_copies:
        for copy in copies:
            copy.wait()


def project(tokens, keep_index, norm_gain, w_qkv):
    rows = WINDOWS * BLOCK
    return pl.pallas_call(
        project_kernel,
        in_specs=[HBM, HBM, HBM, HBM],
        out_specs=HBM,
        out_shape=jax.ShapeDtypeStruct((PLANE, X_COUNT, 2, WINDOWS, SLOT), BF16),
        scratch_shapes=[
            pltpu.VMEM((PLANE, X_COUNT, 2, WINDOWS, SLOT), BF16),
            pltpu.VMEM((D,), F32),
            pltpu.VMEM((BLOCKS, WINDOWS, BLOCK, D), BF16),
            pltpu.VMEM((WINDOWS, PAIRS), jnp.int32),
            pltpu.VMEM((2, 4, 128, D), BF16),
        ]
        + [pltpu.VMEM((rows, D), BF16)] * BLOCKS
        + [pltpu.SemaphoreType.DMA((BLOCKS + 3, WINDOWS))],
        compiler_params=pltpu.CompilerParams(vmem_limit_bytes=LIMIT),
        cost_estimate=pl.CostEstimate(flops=2 * 1024 * 1024 * D, bytes_accessed=14_000_000, transcendentals=0),
    )(tokens, keep_index, norm_gain, w_qkv.reshape(3, 2, HEAD_DIM, D))


BATCH = 4


def attend_kernel(in_ref, out_ref):
    total = PLANE * WINDOWS
    scale = 1.0 / math.sqrt(HEAD_DIM)
    lane = lax.broadcasted_iota(jnp.int32, (total, 128), 1)
    flags = in_ref[:, 0, 0, :, LAST:].astype(F32).reshape(total, 128)
    flags = jnp.where(lane >= FLAG, flags, 0.0).astype(BF16)
    same = lax.dot_general(flags, flags, (((1,), (1,)), ((), ())), preferred_element_type=F32) > 0.5
    me = lax.axis_index("x")

    def store(tile, rows):
        rows = rows.reshape(4, 8, WINDOWS, 128).astype(BF16)
        for y in range(4):
            out_ref[:, y, :, tile * 128:(tile + 1) * 128] = rows[y]

    units = [(d, h) for d in range(X_COUNT) for h in range(2)]
    tails = []
    for first in range(0, 8, BATCH):
        group = units[first:first + BATCH]
        scores, values = [], []
        for d, h in group:
            source = lax.rem(me - d + X_COUNT, X_COUNT)

            def part(i):
                return in_ref[:, source, h, :, i * 128:(i + 1) * 128].astype(F32).reshape(total, 128)

            last = part(3)
            query = jnp.concatenate([part(0), jnp.where(lane < TAIL, last, 0.0)], axis=-1).astype(BF16)
            key = jnp.concatenate([part(1), pltpu.roll(last, 128 - TAIL, 1)], axis=-1).astype(BF16)
            value_tail = jnp.where(lane < TAIL, pltpu.roll(last, 128 - 2 * TAIL, 1), 1.0)
            values.append(jnp.concatenate([part(2), value_tail], axis=-1).astype(BF16))
            scores.append(lax.dot_general(query, key, (((1,), (1,)), ((), ())), preferred_element_type=F32))
        weights = []
        for score in scores:
            score = jnp.where(same, score * scale, -jnp.inf)
            weights.append(jnp.exp(score - jnp.max(score, axis=-1, keepdims=True)).astype(BF16))
        mixes = [jnp.dot(w, v, preferred_element_type=F32) for w, v in zip(weights, values)]
        for (d, h), mixed in zip(group, mixes):
            unit = d * 2 + h
            scaled = mixed * (1.0 / mixed[:, 128 + TAIL:128 + TAIL + 1])
            store(unit, scaled[:, :128])
            tail = scaled[:, 128:]
            place = unit % 4
            if place == 0:
                gathered = tail
            else:
                gathered = jnp.where(lane < place * TAIL, gathered, pltpu.roll(tail, place * TAIL, 1))
            if place == 3:
                tails.append(gathered)
    for i, tail in enumerate(tails):
        store(8 + i, tail)


def attend(received):
    return pl.pallas_call(
        attend_kernel,
        in_specs=[VMEM],
        out_specs=VMEM,
        out_shape=jax.ShapeDtypeStruct((8, 4, WINDOWS, X_COUNT * GROUP), BF16),
        compiler_params=pltpu.CompilerParams(vmem_limit_bytes=48 * 1024 * 1024),
        cost_estimate=pl.CostEstimate(flops=8 * 4 * 256 ** 3, bytes_accessed=2_800_000, transcendentals=8 * 65536),
    )(received)


CHUNK = 512
CHUNKS = D // CHUNK


def finish_kernel(attended_ref, w0, w1, w2a, w2b, w3, tokens_hbm, own_hbm, other_hbm, *scratch):
    w_ref, w_tail_ref, t_ref, x_ref, rows_ref, own_ref, other_ref, sems, out_sems = scratch
    core = lax.axis_index("c")
    first = pl.multiple_of((lax.axis_index("x") * 2 + core) * 16, 16)
    token_copy = pltpu.make_async_copy(tokens_hbm.at[:, pl.ds(first, 16)], t_ref, sems.at[CHUNKS, 0])
    parts = [(w0, 0), (w1, 2), (w2a, 4), (w2b, 5), (w3, 6)]
    copies = [
        [
            pltpu.make_async_copy(
                w.at[:, pl.ds(lo, size), pl.ds(n * CHUNK, CHUNK)],
                to_ref.at[pl.ds(head, w.shape[0]), :, pl.ds(n * CHUNK, CHUNK)],
                sems.at[n, i * 2 + j],
            )
            for i, (w, head) in enumerate(parts)
            for j, (lo, size, to_ref) in enumerate(((0, 128, w_ref), (128, TAIL, w_tail_ref)))
        ]
        for n in range(CHUNKS)
    ]
    for copy in copies[0]:
        copy.start()
    token_copy.start()
    for n in range(1, CHUNKS):
        for copy in copies[n]:
            copy.start()
    for c in range(X_COUNT * GROUP // 128):
        lanes = slice(c * 128, (c + 1) * 128)
        x_ref[c] = attended_ref[:, :, lanes].astype(F32).reshape(PLANE * WINDOWS, 128)
        for half, owner in ((0, core), (1, 1 - core)):
            for w in range(WINDOWS):
                to = half * 128 + w * 16
                picked = [
                    x_ref[c, pl.ds((owner * 2 + y) * WINDOWS + w, 8, stride=4 * WINDOWS), :] for y in range(2)
                ]
                rows_ref[to:to + 16, lanes] = jnp.concatenate(picked, axis=0).astype(BF16)
    out_copies = []
    for n in range(CHUNKS):
        lanes = slice(n * CHUNK, (n + 1) * CHUNK)
        for copy in copies[n]:
            copy.wait()
        total = jnp.dot(
            rows_ref[:, :1024], w_ref[:, :, lanes].reshape(1024, CHUNK), preferred_element_type=F32
        ) + jnp.dot(rows_ref[:, 1024:], w_tail_ref[:, :, lanes].reshape(256, CHUNK), preferred_element_type=F32)
        if n == 0:
            token_copy.wait()
        own = t_ref[:, :, lanes].astype(F32) + total[:128].reshape(WINDOWS, 16, CHUNK)
        own_ref[:, :, lanes] = own.astype(BF16)
        other_ref[:, :, lanes] = total[128:].reshape(WINDOWS, 16, CHUNK).astype(BF16)
        columns = pl.ds(n * CHUNK, CHUNK)
        for i, (ref, hbm) in enumerate(((own_ref, own_hbm), (other_ref, other_hbm))):
            out_copies.append(
                pltpu.make_async_copy(ref.at[:, :, columns], hbm.at[:, :, columns], out_sems.at[n, i])
            )
            out_copies[-1].start()
    for copy in out_copies:
        copy.wait()


def finish(attended, weights, tokens):
    return pl.pallas_call(
        finish_kernel,
        in_specs=[VMEM] + [HBM] * 6,
        out_specs=(HBM, HBM),
        out_shape=(
            jax.ShapeDtypeStruct((WINDOWS, 16, D), BF16),
            jax.ShapeDtypeStruct((WINDOWS, 16, D), BF16),
        ),
        scratch_shapes=[
            pltpu.VMEM((8, 128, D), BF16),
            pltpu.VMEM((8, TAIL, D), BF16),
            pltpu.VMEM((WINDOWS, 16, D), BF16),
            pltpu.VMEM((X_COUNT * GROUP // 128, PLANE * WINDOWS, 128), F32),
            pltpu.VMEM((PLANE * WINDOWS, X_COUNT * GROUP), BF16),
            pltpu.VMEM((WINDOWS, 16, D), BF16),
            pltpu.VMEM((WINDOWS, 16, D), BF16),
            pltpu.SemaphoreType.DMA((CHUNKS + 1, 10)),
            pltpu.SemaphoreType.DMA((CHUNKS, 2)),
        ],
        compiler_params=pltpu.CompilerParams(vmem_limit_bytes=50 * 1024 * 1024),
        cost_estimate=pl.CostEstimate(flops=2 * 256 * 1280 * D, bytes_accessed=9_000_000, transcendentals=0),
    )(attended, *[w.reshape(-1, HEAD_DIM, D) for w in weights], tokens)


def shift(value, axis, by):
    count = lax.axis_size(axis)
    return lax.ppermute(value, axis, [(i, (i + by) % count) for i in range(count)])


def local(tokens, keep_index, norm_gain, w_qkv, w_out):
    w1 = shift(w_out, "x", 1)
    w3 = shift(w_out, "x", -1)
    w2a = shift(w1[:HEAD_DIM], "x", 1)
    w2b = shift(w3[HEAD_DIM:], "x", -1)
    sent = project(tokens, keep_index, norm_gain, w_qkv)
    received = lax.all_to_all(
        sent.reshape(X_COUNT * PLANE, 2 * WINDOWS, SLOT), ("y", "z", "x"), split_axis=0, concat_axis=0, tiled=True
    )
    attended = attend(received.reshape(PLANE, X_COUNT, 2, WINDOWS, SLOT))
    returned = lax.all_to_all(
        attended.reshape(PLANE, WINDOWS, X_COUNT * GROUP), ("z", "y"), split_axis=0, concat_axis=0, tiled=True
    )
    own, other = finish(returned, (w_out, w1, w2a, w2b, w3), tokens)
    return (own.astype(F32) + shift(other, "c", 1).astype(F32)).astype(BF16)


def solution(mesh):
    mesh = Mesh(mesh.devices.reshape(4, 8, 4, 2), ("y", "z", "x", "c"))
    win, pos = ("y", "z"), ("x", "c")
    in_specs = (P(win, None, None), P(win, None), P(), P(None, pos, None), P(pos, None))
    return jax.shard_map(local, mesh=mesh, in_specs=in_specs, out_specs=P(win, pos, None), check_vma=False)
```
